512 devices in a mesh: fsdp: 16 (over z), expert: 32 (over x, y, core).
Axes of the slice: x: 4, y: 4, z: 16, core: 2. Of those that a mesh axis runs over, the one named last changes fastest.
Arguments:
- tokens: bfloat16 [65536, 2048], P(('fsdp', 'expert')), may hold values from -6 to 6
- expert_ids: int32 [65536, 4], P(('fsdp', 'expert')), may hold values from 0 to 63, all different within a row
- priority: int32 [512, 512], P(('fsdp', 'expert')), may hold values from 0 to 511, each once within a row
- overflow_pick: int32 [65536, 4], P(('fsdp', 'expert')), may hold values from 0 to 1
- partner: int32 [32], replicated, may hold values from 0 to 31, each once
- capacity: int32 [64], replicated, may hold values from 4 to 8, as said below
- route_scale: float32 [65536, 4], P(('fsdp', 'expert')), may hold values from 0.05 to 0.5
- gate_weight: bfloat16 [64, 2048, 768], P('expert', 'fsdp'), may hold values from -0.125 to 0.125
- up_weight: bfloat16 [64, 2048, 768], P('expert', 'fsdp'), may hold values from -0.125 to 0.125
- down_weight: bfloat16 [64, 768, 2048], P('expert', None, 'fsdp'), may hold values from -0.21875 to 0.21875
Outputs:
- mixed: bfloat16 [65536, 2048], P(('fsdp', 'expert'))
The draws below stay inside these ranges and needn't reach their ends.
Inputs may be any that keep to these rules, and one draw needn't show every extreme that they name: capacity[e] main slots for each device's rows; at least a quarter of the experts grant exactly 8. `priority`: each row holds every number once. `partner`: each group number once.
All inputs are finite; a program needn't handle non-finite values.
Results may differ from the reference program's by a relative error of at most 0.0058.
Values may be sent and summed in bfloat16 or wider, within the bound.
No kernel may reach another device: no remote copies, remote signals or barrier semaphores. Data moves between devices by JAX's collectives and lax.ppermute only.
A program may use at most 64 MiB of HBM per device.

```python
import math
import jax
import jax.numpy as jnp
from jax import lax

D = 2048
HID = 768
TOP = 4
GROUP = 2
TOK_DEV = 128
EXPERTS = 64
SLOTS = 8
OSLOTS = 2
TOKENS = 65536
N_FSDP = 16
N_EXPERT = 32


def draw_capacity(key, part):
    key = jax.random.fold_in(key, 7)
    key_low, second = jax.random.split(key)
    values = jax.random.randint(key_low, (EXPERTS,), SLOTS // 2, SLOTS + 1)
    ranking = jax.random.permutation(second, EXPERTS)
    forced = ranking < max(EXPERTS // 4, 1)
    return jnp.where(forced, SLOTS, values).astype(jnp.int32)


def touch_ends(entries, key, smallest, top_value):
    spot = [jax.random.randint(jax.random.fold_in(key, axis), (), 0, length) for axis, length in enumerate(entries.shape)]
    longest = entries.shape.index(max(entries.shape))
    next_to = spot[:longest] + [(spot[longest] + 1) % entries.shape[longest]] + spot[longest + 1:]
    return entries.at[tuple(spot)].set(smallest).at[tuple(next_to)].set(top_value)


def block_scale(key, extent, shards, smallest, top_value):
    def one(axis_at, shards_of):
        draws = jax.random.uniform(jax.random.fold_in(jax.random.fold_in(key, 6), axis_at), (shards_of,), jnp.float32, smallest / len(shards), top_value / len(shards))
        return jnp.repeat(jnp.exp(draws), extent[axis_at] // shards_of).reshape((-1,) + (1,) * (len(extent) - axis_at - 1))

    level = one(*shards[0])
    for cut in shards[1:]:
        level = level * one(*cut)
    return level


def choose_distinct(own_key, rows, count, top, lift):
    order = jax.random.permutation(jax.random.fold_in(own_key, 1), count)
    pull = order
    for power in range(3):
        pull = pull * pull // count
    pull = pull * lift // count
    chance = jax.random.randint(jax.random.fold_in(own_key, 2), (rows, count), 0, 4096) + pull
    holders = jax.random.permutation(jax.random.fold_in(own_key, 3), rows)[jnp.arange(count) % rows]
    chance = jnp.where(jnp.arange(rows)[:, None] == holders[None, :], 1 << 14, chance)
    merit = chance * count + jnp.arange(count)
    return lax.top_k(merit.astype(jnp.int32), top)[1].astype(jnp.int32)


def scatter_about(rng, dims, width, bound, cuts=(), kind=jnp.bfloat16):
    drawn = width * jax.random.normal(rng, dims, jnp.float32)
    if cuts:
        drawn = drawn * block_scale(rng, dims, cuts, -0.22, 0.18)
    return jnp.clip(drawn, -bound, bound).astype(kind)


def setup_inputs(seed: int = 0) -> dict:
    key_of = jax.random.split(jax.random.key(seed), 11)
    return {
        "tokens": scatter_about(key_of[0], (TOKENS, D), 1.0, 6.0, ((0, 512),)),
        "expert_ids": choose_distinct(key_of[1], TOKENS, EXPERTS, TOP, 1024),
        "priority": jax.vmap(lambda own: jax.random.permutation(own, TOK_DEV * TOP))(jax.random.split(key_of[2], (N_FSDP * N_EXPERT))).reshape((N_FSDP * N_EXPERT, TOK_DEV * TOP)).astype(jnp.int32),
        "overflow_pick": touch_ends(jax.random.randint(key_of[3], (TOKENS, TOP), 0, GROUP), jax.random.fold_in(key_of[3], 1), 0, GROUP - 1).astype(jnp.int32),
        "partner": jax.random.permutation(key_of[4], EXPERTS // GROUP).astype(jnp.int32),
        "capacity": draw_capacity(jax.random.fold_in(key_of[10], 71), 0),
        "route_scale": jnp.clip(jnp.exp(math.log(0.5) - 2.3025851 * jax.random.uniform(key_of[6], (TOKENS, TOP), jnp.float32) ** block_scale(key_of[6], (TOKENS, TOP), ((0, 512),), -0.2, 0.2)), 0.05, 0.5),
        "gate_weight": scatter_about(key_of[7], (EXPERTS, D, HID), D ** -0.5, 0.125, ((0, 32), (1, 16))),
        "up_weight": scatter_about(key_of[8], (EXPERTS, D, HID), D ** -0.5, 0.125, ((0, 32), (1, 16))),
        "down_weight": scatter_about(key_of[9], (EXPERTS, HID, D), HID ** -0.5, 0.21875, ((0, 32), (2, 16))),
    }


def routing(expert_ids, overflow_pick, order_key, capacity, partner, experts, slot_count, spill_count):
    flat_ids = expert_ids.reshape(-1).astype(jnp.int32)
    flat_pick = overflow_pick.reshape(-1).astype(jnp.int32)
    earlier = order_key[None, :] < order_key[:, None]
    same_expert = flat_ids[None, :] == flat_ids[:, None]
    slot_rank = jnp.sum((same_expert & earlier).astype(jnp.int32), axis=1, dtype=jnp.int32)
    expert_range = jnp.arange(experts, dtype=jnp.int32)
    cap_of = jnp.sum(jnp.where(flat_ids[:, None] == expert_range[None, :], capacity[None, :], 0), axis=1, dtype=jnp.int32)
    kept_main = slot_rank < cap_of
    group_range = jnp.arange(experts // GROUP, dtype=jnp.int32)
    partner_group = jnp.sum(jnp.where((flat_ids // GROUP)[:, None] == group_range[None, :], partner[None, :], 0), axis=1, dtype=jnp.int32)
    target = partner_group * GROUP + flat_pick
    spilled = jnp.logical_not(kept_main)
    same_target = target[None, :] == target[:, None]
    spill_rank = jnp.sum((same_target & earlier & spilled[None, :]).astype(jnp.int32), axis=1, dtype=jnp.int32)
    kept_spill = spilled & (spill_rank < spill_count)
    slot_width = slot_count + spill_count
    position = jnp.where(kept_main, flat_ids * slot_width + slot_rank,
                         jnp.where(kept_spill, target * slot_width + slot_count + spill_rank, experts * slot_width))
    return position.astype(jnp.int32)


def expert_mlp(row_block, gate_w, up_w, down_w):
    gate_sum = jnp.dot(row_block, gate_w, preferred_element_type=jnp.float32)
    up_sum = jnp.dot(row_block, up_w, preferred_element_type=jnp.float32)
    hidden = (jax.nn.silu(gate_sum) * up_sum).astype(jnp.bfloat16)
    return jnp.dot(hidden, down_w, preferred_element_type=jnp.float32).astype(jnp.bfloat16)


def reference(tokens, expert_ids, priority, overflow_pick, partner, capacity, route_scale, gate_weight, up_weight, down_weight):
    blocks = N_FSDP * N_EXPERT
    slot_width = SLOTS + OSLOTS
    choices_dev = TOK_DEV * TOP

    def route_block(ids_block, pick_block, key_block):
        return routing(ids_block, pick_block, key_block, capacity, partner, EXPERTS, SLOTS, OSLOTS)

    position = jax.vmap(route_block)(expert_ids.reshape(blocks, TOK_DEV, TOP), overflow_pick.reshape(blocks, TOK_DEV, TOP), priority)
    owner_token = jnp.arange(choices_dev, dtype=jnp.int32) // TOP
    flat_scale = route_scale.reshape(blocks, choices_dev)

    def fill_block(place, scales):
        slot_token = jnp.full((EXPERTS * slot_width,), -1, jnp.int32).at[place].set(owner_token, mode="drop")
        slot_scale = jnp.zeros((EXPERTS * slot_width,), jnp.float32).at[place].set(scales, mode="drop")
        return slot_token, slot_scale

    slot_token, slot_scale = jax.vmap(fill_block)(position, flat_scale)
    slot_token = slot_token.reshape(blocks, EXPERTS, slot_width).transpose(1, 0, 2)
    slot_scale = slot_scale.reshape(blocks, EXPERTS, slot_width).transpose(1, 0, 2)
    grouped = tokens.reshape(blocks, TOK_DEV, D)
    block_index = jnp.arange(blocks, dtype=jnp.int32)[:, None]

    def one_expert(mixed_sum, inputs):
        token_rows, scale_rows, gate_w, up_w, down_w = inputs
        occupied = token_rows >= 0
        safe_rows = jnp.maximum(token_rows, 0)
        row_block = grouped[block_index, safe_rows]
        row_block = jnp.where(occupied[..., None], row_block, jnp.zeros((), jnp.bfloat16))
        answer = expert_mlp(row_block.reshape(-1, D), gate_w, up_w, down_w).reshape(blocks, slot_width, D)
        weighted = jnp.where(occupied[..., None], scale_rows[..., None] * answer.astype(jnp.float32), jnp.float32(0.0))
        mixed_sum = mixed_sum.at[block_index, safe_rows].add(weighted)
        return mixed_sum, None

    initial = jnp.zeros((blocks, TOK_DEV, D), jnp.float32)
    mixed_sum, _ = lax.scan(one_expert, initial, (slot_token, slot_scale, gate_weight, up_weight, down_weight))
    return mixed_sum.reshape(TOKENS, D).astype(jnp.bfloat16)
```

```python
import jax
import jax.numpy as jnp
from jax import lax
from jax.experimental import pallas as pl
from jax.experimental.pallas import tpu as pltpu
from jax.sharding import PartitionSpec as P

TOP = 4
GROUP = 2
LANE = 128
VMEM_LIMIT = 56 * 1024 * 1024

TOK = 128
CHOICES = TOK * TOP
EXPERTS = 64
SLOTS = 8
OSLOTS = 2
DEVICES = 32
MAIN = EXPERTS * SLOTS
SPILL = EXPERTS * OSLOTS
ROWS = MAIN + SPILL
D = 2048
HID = 768
PIECES = 16
PIECE = 3 * LANE
HALF = PIECE // 2


def iota(shape, axis):
    return lax.broadcasted_iota(jnp.int32, shape, axis)


def ones_where(hit):
    return jnp.where(hit, 1, 0)


def spill_index(row):
    return (row >> 4) * 4 + (row & 3)


def spill_quarter(row):
    return (row >> 2) & 3


def one_hot(hit):
    return jnp.where(hit, 1.0, 0.0).astype(jnp.bfloat16)


def dot(a, b):
    return jnp.dot(a, b, preferred_element_type=jnp.float32)


def across(a, b):
    return lax.dot_general(a, b, (((1,), (1,)), ((), ())), preferred_element_type=jnp.float32)


MAIN_E = MAIN // 2
SPILL_E = SPILL // 2
ROWS_E = ROWS // 2


def dispatch_kernel(
    rows, cols, partner_r, partner_c, cap_r, cap_c, scale, tokens, out, s_hi, s_lo, p_hi, p_lo,
):
    ids_r, key_r, pick_r = rows[0:1, :], rows[1:2, :], rows[2:3, :]
    rank_r = jnp.zeros((1, CHOICES), jnp.int32)
    rank_c = []
    for b in range(TOP):
        at = slice(b * TOK, (b + 1) * TOK)
        ids_c, key_c = cols[at, 0:1], cols[at, 1:2]
        same = ids_c == ids_r
        rank_r += jnp.sum(ones_where(same & (key_c < key_r)), axis=0, keepdims=True)
        rank_c.append(jnp.sum(ones_where(same & (key_r < key_c)), axis=1, keepdims=True))
    room_r = jnp.sum(jnp.where(iota((EXPERTS, CHOICES), 0) == ids_r, cap_c[...], 0), axis=0, keepdims=True)
    mate_r = jnp.sum(
        jnp.where(iota((EXPERTS // GROUP, CHOICES), 0) == (ids_r >> 1), partner_c[...], 0), axis=0, keepdims=True
    )
    target_r = mate_r * GROUP + pick_r
    over_r = ones_where(rank_r >= room_r)
    spill_r = jnp.zeros((1, CHOICES), jnp.int32)
    main_c, lost_c = [], []
    for b in range(TOP):
        at = slice(b * TOK, (b + 1) * TOK)
        ids_c, key_c, pick_c = cols[at, 0:1], cols[at, 1:2], cols[at, 2:3]
        room_c = jnp.sum(jnp.where(iota((TOK, EXPERTS), 1) == ids_c, cap_r[...], 0), axis=1, keepdims=True)
        mate_c = jnp.sum(
            jnp.where(iota((TOK, EXPERTS // GROUP), 1) == (ids_c >> 1), partner_r[...], 0), axis=1, keepdims=True
        )
        target_c = mate_c * GROUP + pick_c
        over_c = ones_where(rank_c[b] >= room_c)
        same = target_c == target_r
        spill_r += jnp.sum(jnp.where(same & (key_c < key_r), over_c, 0), axis=0, keepdims=True)
        spill_c = jnp.sum(jnp.where(same & (key_r < key_c), over_r, 0), axis=1, keepdims=True)
        main_c.append(jnp.where(over_c == 0, ids_c * SLOTS + rank_c[b], -1))
        lost_c.append(jnp.where((over_c == 1) & (spill_c < OSLOTS), target_c * OSLOTS + spill_c, -1))
    main_r = jnp.where(over_r == 0, ids_r * SLOTS + rank_r, -1)
    lost_r = jnp.where((over_r == 1) & (spill_r < OSLOTS), target_r * OSLOTS + spill_r, -1)

    s_main = jnp.zeros((TOK, MAIN), jnp.float32)
    s_lost = jnp.zeros((TOK, MAIN), jnp.float32)
    lane = iota((TOK, MAIN), 1)
    second, own = lane >> 8, lane & (MAIN_E - 1)
    main_of = (own >> 3) * 16 + second * SLOTS + (own & 7)
    lost_of = (own >> 3) * 4 + second * OSLOTS + (own & 1)
    pick_main = jnp.zeros((MAIN, TOK), jnp.float32)
    pick_lost = jnp.zeros((MAIN, TOK), jnp.float32)
    line = iota((MAIN, TOK), 0)
    for k in range(TOP):
        at = slice(k * TOK, (k + 1) * TOK)
        weight = scale[:, k : k + 1]
        s_main += jnp.where(main_of == main_c[k], weight, 0.0)
        s_lost += jnp.where(lost_of == lost_c[k], weight, 0.0)
        pick_main += jnp.where(line == main_r[:, at], 1.0, 0.0)
        pick_lost += jnp.where(spill_index(line) == lost_r[:, at], 1.0, 0.0)
    for value, high, low in ((s_main, s_hi, s_lo), (s_lost, p_hi, p_lo)):
        top = value.astype(jnp.bfloat16)
        high[...] = top
        low[...] = (value - top.astype(jnp.float32)).astype(jnp.bfloat16)

    picks = pick_main.astype(jnp.bfloat16)
    quarter = D // 4
    packed = jnp.zeros((MAIN, quarter), jnp.float32)
    for q in range(4):
        at = slice(q * quarter, (q + 1) * quarter)
        piece = tokens[:, at]
        out[:, at] = jnp.dot(picks, piece, preferred_element_type=jnp.float32).astype(jnp.bfloat16)
        own = jnp.where(spill_quarter(line) == q, pick_lost, 0.0).astype(jnp.bfloat16)
        packed += jnp.dot(own, piece, preferred_element_type=jnp.float32)
    out[:, D:] = packed.astype(jnp.bfloat16)


def main_line(row, e):
    return (row >> 3) * 16 + e * SLOTS + (row & 7)


def packed_line(row, e, q):
    return (row >> 1) * 16 + q * 4 + e * OSLOTS + (row & 1)


def split_kernel(x, out):
    quarter = D // 4
    for e in range(2):
        shape = (MAIN_E, MAIN)
        pick = one_hot(iota(shape, 1) == main_line(iota(shape, 0), e))
        shape = (SPILL_E, MAIN)
        for q in range(4):
            at = slice(q * quarter, (q + 1) * quarter)
            out[e, :MAIN_E, at] = dot(pick, x[:, at]).astype(jnp.bfloat16)
            own = one_hot(iota(shape, 1) == packed_line(iota(shape, 0), e, q))
            out[e, MAIN_E:, at] = dot(own, x[:, D:]).astype(jnp.bfloat16)


def pack_kernel(gate, up, down, first, high, low):
    first[:LANE, :] = gate[0]
    first[LANE : 2 * LANE, :] = up[0]
    first[2 * LANE :, :] = down[0].T
    high[:LANE, :] = gate[1]
    high[LANE:, :] = up[1, : HALF - LANE]
    low[: HALF - LANE, :] = up[1, HALF - LANE :]
    low[HALF - LANE :, :] = down[1].T


WIDE = 2 * LANE
TILES = HID // WIDE


def expert(x, out, gate_w, up_w, down_w, hidden_s, copies):
    for group in copies:
        for copy in group:
            copy.start()
    for n in range(TILES):
        for copy in copies[n]:
            copy.wait()
        cut = slice(n * WIDE, (n + 1) * WIDE)
        gate = dot(x[...], gate_w[:, :, cut].reshape(D, WIDE))
        up = dot(x[...], up_w[:, :, cut].reshape(D, WIDE))
        hidden_s[:, cut] = ((gate / (1.0 + jnp.exp(-gate))) * up).astype(jnp.bfloat16)
    quarter = D // 4
    shape = (MAIN_E, SPILL_E)
    line, row = iota(shape, 0), iota(shape, 1)
    packed = jnp.zeros((MAIN_E, quarter), jnp.float32)
    for q in range(4):
        for copy in copies[TILES + q]:
            copy.wait()
        at = slice(q * quarter, (q + 1) * quarter)
        answer = across(hidden_s[...], down_w[q * 4 : (q + 1) * 4].reshape(quarter, HID)).astype(jnp.bfloat16)
        out[:, at] = answer[:MAIN_E]
        place = one_hot((((line >> 3) * 2 + (line & 1)) == row) & (((line >> 1) & 3) == q))
        packed += dot(place, answer[MAIN_E:])
    out[:, D:] = packed.astype(jnp.bfloat16)


def first_kernel(x, weights, out, gate_w, up_w, down_w, hidden_s, rows, sems, sem):
    copies = [[pltpu.make_async_copy(x.at[0], rows, sem)]] + [[] for _ in range(TILES + 3)]
    for n in range(TILES):
        cut = pl.ds(n * WIDE, WIDE)
        for i, to in enumerate((gate_w, up_w)):
            source = weights.at[:, pl.ds(i * LANE, LANE), cut]
            copies[n].append(pltpu.make_async_copy(source, to.at[:, :, cut], sems.at[i, n]))
    for q in range(4):
        own = pl.ds(q * 4, 4)
        source = weights.at[own, pl.ds(2 * LANE, LANE)]
        copies[TILES + q].append(pltpu.make_async_copy(source, down_w.at[own], sems.at[2, q]))
    expert(rows, out, gate_w, up_w, down_w, hidden_s, copies)


def second_kernel(me, x, *refs):
    highs, lows = refs[:PIECES], refs[PIECES : 2 * PIECES]
    out, gate_w, up_w, down_w, hidden_s, sems = refs[2 * PIECES :]
    copies = [[] for _ in range(TILES + 4)]
    half = HALF - LANE
    for j in range(PIECES):
        owner = lax.rem(me[0] + j, PIECES)
        moves = [
            (highs[j].at[pl.ds(0, LANE)], gate_w.at[owner]),
            (highs[j].at[pl.ds(LANE, half)], up_w.at[owner, pl.ds(0, half)]),
            (lows[j].at[pl.ds(0, half)], up_w.at[owner, pl.ds(half, half)]),
            (lows[j].at[pl.ds(half, LANE)], down_w.at[owner]),
        ]
        now = [pltpu.make_async_copy(source, to, sems.at[i, j]) for i, (source, to) in enumerate(moves)]
        copies[0] += now[:-1]
        copies[TILES] += now[-1:]
    expert(x.at[1], out, gate_w, up_w, down_w, hidden_s, copies)


def mix(e, ans, s_hi, s_lo, p_hi, p_lo):
    own = slice(e * MAIN_E, (e + 1) * MAIN_E)
    both = jnp.concatenate([s_hi[:, own], s_lo[:, own]], axis=0)
    total = dot(both, ans[:, :D])
    total = total[:TOK] + total[TOK:]
    both = jnp.concatenate([p_hi[:, own], p_lo[:, own]], axis=0)
    quarter = (iota(both.shape, 1) >> 1) & 3
    zero = jnp.zeros((), jnp.bfloat16)
    sums = []
    for q in range(4):
        lost = dot(jnp.where(quarter == q, both, zero), ans[:, D:])
        sums.append(lost[:TOK] + lost[TOK:])
    return total + jnp.concatenate(sums, axis=1)


def mix_kernel(ans, s_hi, s_lo, p_hi, p_lo, out):
    out[...] = mix(1, ans, s_hi, s_lo, p_hi, p_lo)


def final_kernel(ans, s_hi, s_lo, p_hi, p_lo, before, out):
    out[...] = (before[...] + mix(0, ans, s_hi, s_lo, p_hi, p_lo)).astype(jnp.bfloat16)


def params():
    return pltpu.CompilerParams(vmem_limit_bytes=VMEM_LIMIT)


def vmem(count):
    return [pl.BlockSpec(memory_space=pltpu.VMEM)] * count


def anywhere(count):
    return [pl.BlockSpec(memory_space=pl.ANY)] * count


SMEM = pl.BlockSpec(memory_space=pltpu.SMEM)


def cost(flops, size):
    return pl.CostEstimate(flops=flops, bytes_accessed=size, transcendentals=0)


def dispatch(expert_ids, priority, overflow_pick, partner, capacity, route_scale, tokens):
    def by_choice(block):
        return block.reshape(TOK, TOP).T.reshape(1, CHOICES)

    rows = jnp.concatenate([by_choice(expert_ids), by_choice(priority), by_choice(overflow_pick)], axis=0)
    scales = jax.ShapeDtypeStruct((TOK, MAIN), jnp.bfloat16)
    return pl.pallas_call(
        dispatch_kernel,
        out_shape=[jax.ShapeDtypeStruct((MAIN, D + D // 4), jnp.bfloat16)] + [scales] * 4,
        in_specs=vmem(8),
        out_specs=vmem(5),
        compiler_params=params(),
        cost_estimate=cost(2 * MAIN * TOK * D * 2, 4 * 1024 * 1024),
    )(
        rows, rows.T, partner[None, :], partner[:, None], capacity[None, :], capacity[:, None],
        route_scale, tokens,
    )


def pack(gate_weight, up_weight, down_weight):
    half = jax.ShapeDtypeStruct((HALF, HID), jnp.bfloat16)
    return pl.pallas_call(
        pack_kernel,
        out_shape=[jax.ShapeDtypeStruct((PIECE, HID), jnp.bfloat16), half, half],
        in_specs=vmem(3),
        out_specs=vmem(3),
        compiler_params=params(),
        cost_estimate=cost(0, 8 * PIECE * HID),
    )(gate_weight, up_weight, down_weight)


def split_rows(x):
    return pl.pallas_call(
        split_kernel,
        out_shape=jax.ShapeDtypeStruct((2, ROWS_E, D), jnp.bfloat16),
        in_specs=vmem(1),
        out_specs=vmem(1)[0],
        compiler_params=params(),
        cost_estimate=cost(2 * ROWS * MAIN * D, 6 * 1024 * 1024),
    )(x)


def expert_scratch():
    return [pltpu.VMEM((PIECES, LANE, HID), jnp.bfloat16)] * 3 + [pltpu.VMEM((ROWS_E, HID), jnp.bfloat16)]


EXPERT_OUT = jax.ShapeDtypeStruct((MAIN_E, D + D // 4), jnp.bfloat16)
EXPERT_COST = cost(6 * ROWS_E * D * HID, 13 * 1024 * 1024)


def first_expert(x, weights):
    return pl.pallas_call(
        first_kernel,
        out_shape=EXPERT_OUT,
        in_specs=anywhere(2),
        out_specs=vmem(1)[0],
        scratch_shapes=[
            *expert_scratch(),
            pltpu.VMEM((ROWS_E, D), jnp.bfloat16),
            pltpu.SemaphoreType.DMA((3, 4)),
            pltpu.SemaphoreType.DMA,
        ],
        compiler_params=params(),
        cost_estimate=EXPERT_COST,
    )(x, weights)


def second_expert(me, x, pieces):
    return pl.pallas_call(
        second_kernel,
        out_shape=EXPERT_OUT,
        in_specs=[SMEM] + vmem(1) + anywhere(len(pieces)),
        out_specs=vmem(1)[0],
        scratch_shapes=[*expert_scratch(), pltpu.SemaphoreType.DMA((4, PIECES))],
        compiler_params=params(),
        cost_estimate=EXPERT_COST,
    )(me, x, *pieces)


def combine(ans, scales):
    return pl.pallas_call(
        mix_kernel,
        out_shape=jax.ShapeDtypeStruct((TOK, D), jnp.float32),
        in_specs=vmem(5),
        out_specs=vmem(1)[0],
        compiler_params=params(),
        cost_estimate=cost(5 * TOK * MAIN_E * D, 3 * 1024 * 1024),
    )(ans, *scales)


def combine_last(ans, scales, before):
    return pl.pallas_call(
        final_kernel,
        out_shape=jax.ShapeDtypeStruct((TOK, D), jnp.bfloat16),
        in_specs=vmem(6),
        out_specs=vmem(1)[0],
        compiler_params=params(),
        cost_estimate=cost(5 * TOK * MAIN_E * D, 3 * 1024 * 1024),
    )(ans, *scales, before)


def exchange(block):
    rows, width = block.shape
    shaped = block.reshape(DEVICES, rows // DEVICES, width)
    return lax.all_to_all(shaped, "expert", split_axis=0, concat_axis=0, tiled=True).reshape(rows, width)


def after(value, *others):
    return lax.optimization_barrier((value, *others))[0]


def per_device(
    tokens, expert_ids, priority, overflow_pick, partner, capacity, route_scale,
    gate_weight, up_weight, down_weight,
):
    me = lax.axis_index("fsdp").astype(jnp.int32).reshape(1)
    right = [(i, (i + 1) % PIECES) for i in range(PIECES)]
    left = [(i, (i - 1) % PIECES) for i in range(PIECES)]

    own, high, low = pack(gate_weight, up_weight, down_weight)
    weights = lax.all_gather(own, "fsdp")
    highs, lows = {0: high}, {0: low}
    half = PIECES // 2
    for step in range(1, half + 1):
        highs[PIECES - step] = lax.ppermute(highs[(PIECES - step + 1) % PIECES], "fsdp", right)
        lows[step] = lax.ppermute(lows[step - 1], "fsdp", left)
        if step < half:
            highs[step] = lax.ppermute(highs[step - 1], "fsdp", left)
            lows[PIECES - step] = lax.ppermute(lows[(PIECES - step + 1) % PIECES], "fsdp", right)
    pieces = [highs[j] for j in range(PIECES)] + [lows[j] for j in range(PIECES)]

    ready = after(tokens, highs[PIECES - 1], lows[1])
    out, *scales = dispatch(expert_ids, priority, overflow_pick, partner, capacity, route_scale, ready)
    x = split_rows(exchange(out))
    second = second_expert(me, x, pieces)
    first = first_expert(after(x, second), weights)
    before = combine(exchange(second), scales)
    return combine_last(exchange(first), scales, before)


def solution(mesh):
    in_specs = (
        P(("fsdp", "expert"), None),
        P(("fsdp", "expert"), None),
        P(("fsdp", "expert"), None),
        P(("fsdp", "expert"), None),
        P(),
        P(),
        P(("fsdp", "expert"), None),
        P("expert", "fsdp", None),
        P("expert", "fsdp", None),
        P("expert", None, "fsdp"),
    )
    out_specs = P(("fsdp", "expert"), None)
    return jax.shard_map(
        per_device, mesh=mesh, in_specs=in_specs, out_specs=out_specs, check_vma=False
    )
```

```python
import functools

import jax
import jax.numpy as jnp
from jax import lax
from jax.experimental import pallas as pl
from jax.experimental.pallas import tpu as pltpu
from jax.sharding import PartitionSpec as P

TOP = 4
GROUP = 2
LANE = 128
VMEM_LIMIT = 56 * 1024 * 1024
SMALL_LIMIT = 24 * 1024 * 1024

TOK = 128
CHOICES = TOK * TOP
EXPERTS = 64
SLOTS = 8
OSLOTS = 2
DEVICES = 32
MAIN = EXPERTS * SLOTS
SPILL = EXPERTS * OSLOTS
ROWS = MAIN + SPILL
D = 2048
HID = 768
PIECES = 16
PIECE = 3 * LANE
HALF = PIECE // 2
LAG = 0
XSTEP = 6
KSTEP = 4


def iota(shape, axis):
    return lax.broadcasted_iota(jnp.int32, shape, axis)


def ones_where(hit):
    return jnp.where(hit, 1, 0)


def spill_index(row):
    return (row >> 4) * 4 + (row & 3)


def spill_quarter(row):
    return (row >> 2) & 3


def one_hot(hit):
    return jnp.where(hit, 1.0, 0.0).astype(jnp.bfloat16)


def dot(a, b):
    return jnp.dot(a, b, preferred_element_type=jnp.float32)


def across(a, b):
    return lax.dot_general(a, b, (((1,), (1,)), ((), ())), preferred_element_type=jnp.float32)


MAIN_E = MAIN // 2
SPILL_E = SPILL // 2
ROWS_E = ROWS // 2


def dispatch_kernel(
    rows, cols, partner_r, partner_c, cap_r, cap_c, scale, tokens, out, s_hi, s_lo, p_hi, p_lo,
):
    ids_r, key_r, pick_r = rows[0:1, :], rows[1:2, :], rows[2:3, :]
    rank_r = jnp.zeros((1, CHOICES), jnp.int32)
    rank_c = []
    for b in range(TOP):
        at = slice(b * TOK, (b + 1) * TOK)
        ids_c, key_c = cols[at, 0:1], cols[at, 1:2]
        same = ids_c == ids_r
        rank_r += jnp.sum(ones_where(same & (key_c < key_r)), axis=0, keepdims=True)
        rank_c.append(jnp.sum(ones_where(same & (key_r < key_c)), axis=1, keepdims=True))
    room_r = jnp.sum(jnp.where(iota((EXPERTS, CHOICES), 0) == ids_r, cap_c[...], 0), axis=0, keepdims=True)
    mate_r = jnp.sum(
        jnp.where(iota((EXPERTS // GROUP, CHOICES), 0) == (ids_r >> 1), partner_c[...], 0), axis=0, keepdims=True
    )
    target_r = mate_r * GROUP + pick_r
    over_r = ones_where(rank_r >= room_r)
    spill_r = jnp.zeros((1, CHOICES), jnp.int32)
    main_c, lost_c = [], []
    for b in range(TOP):
        at = slice(b * TOK, (b + 1) * TOK)
        ids_c, key_c, pick_c = cols[at, 0:1], cols[at, 1:2], cols[at, 2:3]
        room_c = jnp.sum(jnp.where(iota((TOK, EXPERTS), 1) == ids_c, cap_r[...], 0), axis=1, keepdims=True)
        mate_c = jnp.sum(
            jnp.where(iota((TOK, EXPERTS // GROUP), 1) == (ids_c >> 1), partner_r[...], 0), axis=1, keepdims=True
        )
        target_c = mate_c * GROUP + pick_c
        over_c = ones_where(rank_c[b] >= room_c)
        same = target_c == target_r
        spill_r += jnp.sum(jnp.where(same & (key_c < key_r), over_c, 0), axis=0, keepdims=True)
        spill_c = jnp.sum(jnp.where(same & (key_r < key_c), over_r, 0), axis=1, keepdims=True)
        main_c.append(jnp.where(over_c == 0, ids_c * SLOTS + rank_c[b], -1))
        lost_c.append(jnp.where((over_c == 1) & (spill_c < OSLOTS), target_c * OSLOTS + spill_c, -1))
    main_r = jnp.where(over_r == 0, ids_r * SLOTS + rank_r, -1)
    lost_r = jnp.where((over_r == 1) & (spill_r < OSLOTS), target_r * OSLOTS + spill_r, -1)

    s_main = jnp.zeros((TOK, MAIN), jnp.float32)
    s_lost = jnp.zeros((TOK, MAIN), jnp.float32)
    lane = iota((TOK, MAIN), 1)
    second, own = lane >> 8, lane & (MAIN_E - 1)
    main_of = (own >> 3) * 16 + second * SLOTS + (own & 7)
    lost_of = (own >> 3) * 4 + second * OSLOTS + (own & 1)
    pick_main = jnp.zeros((MAIN, TOK), jnp.float32)
    pick_lost = jnp.zeros((MAIN, TOK), jnp.float32)
    line = iota((MAIN, TOK), 0)
    for k in range(TOP):
        at = slice(k * TOK, (k + 1) * TOK)
        weight = scale[:, k : k + 1]
        s_main += jnp.where(main_of == main_c[k], weight, 0.0)
        s_lost += jnp.where(lost_of == lost_c[k], weight, 0.0)
        pick_main += jnp.where(line == main_r[:, at], 1.0, 0.0)
        pick_lost += jnp.where(spill_index(line) == lost_r[:, at], 1.0, 0.0)
    for value, high, low in ((s_main, s_hi, s_lo), (s_lost, p_hi, p_lo)):
        top = value.astype(jnp.bfloat16)
        high[...] = top
        low[...] = (value - top.astype(jnp.float32)).astype(jnp.bfloat16)

    picks = pick_main.astype(jnp.bfloat16)
    quarter = D // 4
    packed = jnp.zeros((MAIN, quarter), jnp.float32)
    for q in range(4):
        at = slice(q * quarter, (q + 1) * quarter)
        piece = tokens[:, at]
        out[:, at] = jnp.dot(picks, piece, preferred_element_type=jnp.float32).astype(jnp.bfloat16)
        own = jnp.where(spill_quarter(line) == q, pick_lost, 0.0).astype(jnp.bfloat16)
        packed += jnp.dot(own, piece, preferred_element_type=jnp.float32)
    out[:, D:] = packed.astype(jnp.bfloat16)


def main_line(row, e):
    return (row >> 3) * 16 + e * SLOTS + (row & 7)


def packed_line(row, e, q):
    return (row >> 1) * 16 + q * 4 + e * OSLOTS + (row & 1)


def split_kernel(x, out):
    quarter = D // 4
    for e in range(2):
        shape = (MAIN_E, MAIN)
        pick = one_hot(iota(shape, 1) == main_line(iota(shape, 0), e))
        shape = (SPILL_E, MAIN)
        for q in range(4):
            at = slice(q * quarter, (q + 1) * quarter)
            out[e, :MAIN_E, at] = dot(pick, x[:, at]).astype(jnp.bfloat16)
            own = one_hot(iota(shape, 1) == packed_line(iota(shape, 0), e, q))
            out[e, MAIN_E:, at] = dot(own, x[:, D:]).astype(jnp.bfloat16)


def pack_kernel(gate, up, down, *outs):
    for e, out in enumerate(outs):
        out[:LANE, :] = gate[e]
        out[LANE : 2 * LANE, :] = up[e]
        out[2 * LANE :, :] = down[e].T


WIDE = 2 * LANE
TILES = HID // WIDE


def expert(x, out, gate_w, up_w, down_w, hidden_s, copies):
    for group in copies:
        for copy in group:
            copy.start()
    for n in range(TILES):
        for copy in copies[n]:
            copy.wait()
        cut = slice(n * WIDE, (n + 1) * WIDE)
        gate = dot(x[...], gate_w[:, :, cut].reshape(D, WIDE))
        up = dot(x[...], up_w[:, :, cut].reshape(D, WIDE))
        hidden_s[:, cut] = ((gate / (1.0 + jnp.exp(-gate))) * up).astype(jnp.bfloat16)
    quarter = D // 4
    shape = (MAIN_E, SPILL_E)
    line, row = iota(shape, 0), iota(shape, 1)
    packed = jnp.zeros((MAIN_E, quarter), jnp.float32)
    for q in range(4):
        for copy in copies[TILES + q]:
            copy.wait()
        at = slice(q * quarter, (q + 1) * quarter)
        answer = across(hidden_s[...], down_w[q * 4 : (q + 1) * 4].reshape(quarter, HID)).astype(jnp.bfloat16)
        out[:, at] = answer[:MAIN_E]
        place = one_hot((((line >> 3) * 2 + (line & 1)) == row) & (((line >> 1) & 3) == q))
        packed += dot(place, answer[MAIN_E:])
    out[:, D:] = packed.astype(jnp.bfloat16)


def expert_kernel(e, me, x, *refs):
    pieces, high, low = refs[: PIECES - 1], refs[PIECES - 1], refs[PIECES]
    out, gate_w, up_w, down_w, hidden_s, rows, sems, sem = refs[PIECES + 1 :]
    copies = [[pltpu.make_async_copy(x.at[e], rows, sem)]] + [[] for _ in range(TILES + 3)]
    half = HALF - LANE
    for j in range(PIECES):
        owner = lax.rem(me[0] + j, PIECES)
        if j == PIECES // 2:
            moves = [
                (high.at[pl.ds(0, LANE)], gate_w.at[owner]),
                (high.at[pl.ds(LANE, half)], up_w.at[owner, pl.ds(0, half)]),
                (low.at[pl.ds(0, half)], up_w.at[owner, pl.ds(half, half)]),
                (low.at[pl.ds(half, LANE)], down_w.at[owner]),
            ]
        else:
            piece = pieces[j if j < PIECES // 2 else j - 1]
            moves = [(piece.at[pl.ds(i * LANE, LANE)], to.at[owner]) for i, to in enumerate((gate_w, up_w, down_w))]
        now = [pltpu.make_async_copy(source, to, sems.at[i, j]) for i, (source, to) in enumerate(moves)]
        copies[0] += now[:-1]
        copies[TILES] += now[-1:]
    expert(rows, out, gate_w, up_w, down_w, hidden_s, copies)


def mix(e, ans, s_hi, s_lo, p_hi, p_lo):
    own = slice(e * MAIN_E, (e + 1) * MAIN_E)
    both = jnp.concatenate([s_hi[:, own], s_lo[:, own]], axis=0)
    total = dot(both, ans[:, :D])
    total = total[:TOK] + total[TOK:]
    both = jnp.concatenate([p_hi[:, own], p_lo[:, own]], axis=0)
    quarter = (iota(both.shape, 1) >> 1) & 3
    zero = jnp.zeros((), jnp.bfloat16)
    sums = []
    for q in range(4):
        lost = dot(jnp.where(quarter == q, both, zero), ans[:, D:])
        sums.append(lost[:TOK] + lost[TOK:])
    return total + jnp.concatenate(sums, axis=1)


def final_kernel(first, second, s_hi, s_lo, p_hi, p_lo, out):
    scales = (s_hi, s_lo, p_hi, p_lo)
    out[...] = (mix(0, first, *scales) + mix(1, second, *scales)).astype(jnp.bfloat16)


def params(size=SMALL_LIMIT):
    return pltpu.CompilerParams(vmem_limit_bytes=size)


def vmem(count):
    return [pl.BlockSpec(memory_space=pltpu.VMEM)] * count


def anywhere(count):
    return [pl.BlockSpec(memory_space=pl.ANY)] * count


SMEM = pl.BlockSpec(memory_space=pltpu.SMEM)


def cost(flops, size):
    return pl.CostEstimate(flops=flops, bytes_accessed=size, transcendentals=0)


def dispatch(expert_ids, priority, overflow_pick, partner, capacity, route_scale, tokens):
    def by_choice(block):
        return block.reshape(TOK, TOP).T.reshape(1, CHOICES)

    rows = jnp.concatenate([by_choice(expert_ids), by_choice(priority), by_choice(overflow_pick)], axis=0)
    scales = jax.ShapeDtypeStruct((TOK, MAIN), jnp.bfloat16)
    return pl.pallas_call(
        dispatch_kernel,
        out_shape=[jax.ShapeDtypeStruct((MAIN, D + D // 4), jnp.bfloat16)] + [scales] * 4,
        in_specs=vmem(8),
        out_specs=vmem(5),
        compiler_params=params(),
        cost_estimate=cost(2 * MAIN * TOK * D * 2, 4 * 1024 * 1024),
    )(
        rows, rows.T, partner[None, :], partner[:, None], capacity[None, :], capacity[:, None],
        route_scale, tokens,
    )


def pack(gate_weight, up_weight, down_weight):
    part = jax.ShapeDtypeStruct((PIECE, HID), jnp.bfloat16)
    return pl.pallas_call(
        pack_kernel,
        out_shape=[part, part],
        in_specs=vmem(3),
        out_specs=vmem(2),
        compiler_params=params(VMEM_LIMIT),
        cost_estimate=cost(0, 8 * PIECE * HID),
    )(gate_weight, up_weight, down_weight)


def split_rows(x):
    return pl.pallas_call(
        split_kernel,
        out_shape=jax.ShapeDtypeStruct((2, ROWS_E, D), jnp.bfloat16),
        in_specs=vmem(1),
        out_specs=vmem(1)[0],
        compiler_params=params(),
        cost_estimate=cost(2 * ROWS * MAIN * D, 6 * 1024 * 1024),
    )(x)


def expert_answers(e, me, x, pieces):
    return pl.pallas_call(
        functools.partial(expert_kernel, e),
        out_shape=jax.ShapeDtypeStruct((MAIN_E, D + D // 4), jnp.bfloat16),
        in_specs=[SMEM] + anywhere(1 + len(pieces)),
        out_specs=vmem(1)[0],
        scratch_shapes=[pltpu.VMEM((PIECES, LANE, HID), jnp.bfloat16)] * 3
        + [
            pltpu.VMEM((ROWS_E, HID), jnp.bfloat16),
            pltpu.VMEM((ROWS_E, D), jnp.bfloat16),
            pltpu.SemaphoreType.DMA((4, PIECES)),
            pltpu.SemaphoreType.DMA,
        ],
        compiler_params=params(VMEM_LIMIT),
        cost_estimate=cost(6 * ROWS_E * D * HID, 13 * 1024 * 1024),
    )(me, x, *pieces)


def combine(first, second, scales):
    return pl.pallas_call(
        final_kernel,
        out_shape=jax.ShapeDtypeStruct((TOK, D), jnp.bfloat16),
        in_specs=vmem(6),
        out_specs=vmem(1)[0],
        compiler_params=params(),
        cost_estimate=cost(5 * TOK * MAIN * D, 4 * 1024 * 1024),
    )(first, second, *scales)


def exchange(block):
    rows, width = block.shape
    shaped = block.reshape(DEVICES, rows // DEVICES, width)
    return lax.all_to_all(shaped, "expert", split_axis=0, concat_axis=0, tiled=True).reshape(rows, width)


def after(value, *others):
    return lax.optimization_barrier((value, *others))[0]


def per_device(
    tokens, expert_ids, priority, overflow_pick, partner, capacity, route_scale,
    gate_weight, up_weight, down_weight,
):
    me = lax.axis_index("fsdp").astype(jnp.int32).reshape(1)
    right = [(i, (i + 1) % PIECES) for i in range(PIECES)]
    left = [(i, (i - 1) % PIECES) for i in range(PIECES)]

    ring = [{0: own} for own in pack(gate_weight, up_weight, down_weight)]
    half = PIECES // 2
    for turn in range(1, half + LAG + 1):
        for e in range(2):
            step = turn - e * LAG
            if not 1 <= step <= half:
                continue
            piece = ring[e]
            near_r, near_l = piece[(PIECES - step + 1) % PIECES], piece[step - 1]
            if e == 0 and step == KSTEP:
                out, *scales = dispatch(
                    expert_ids, priority, overflow_pick, partner, capacity, route_scale, after(tokens, near_r)
                )
                x = split_rows(exchange(out))
            if e == 1 and step == XSTEP:
                near_r, near_l = after(near_r, x), after(near_l, x)
            if e == 1 and step == 1 and LAG:
                near_r = after(near_r, ring[0][(PIECES - turn + 1) % PIECES])
                near_l = after(near_l, ring[0][turn - 1])
            if step < half:
                piece[PIECES - step] = lax.ppermute(near_r, "fsdp", right)
                piece[step] = lax.ppermute(near_l, "fsdp", left)
            else:
                high = lax.ppermute(near_r[:HALF], "fsdp", right)
                low = lax.ppermute(near_l[HALF:], "fsdp", left)
                piece[half] = (high, low)
    pieces = [[piece[j] for j in range(PIECES) if j != half] + list(piece[half]) for piece in ring]

    first, second = (exchange(expert_answers(e, me, x, pieces[e])) for e in range(2))
    return combine(first, second, scales)


def solution(mesh):
    in_specs = (
        P(("fsdp", "expert"), None),
        P(("fsdp", "expert"), None),
        P(("fsdp", "expert"), None),
        P(("fsdp", "expert"), None),
        P(),
        P(),
        P(("fsdp", "expert"), None),
        P("expert", "fsdp", None),
        P("expert", "fsdp", None),
        P("expert", None, "fsdp"),
    )
    out_specs = P(("fsdp", "expert"), None)
    return jax.shard_map(
        per_device, mesh=mesh, in_specs=in_specs, out_specs=out_specs, check_vma=False
    )
```

```python
import jax
import jax.numpy as jnp
from jax import lax
from jax.experimental import pallas as pl
from jax.experimental.pallas import tpu as pltpu
from jax.sharding import PartitionSpec as P

TOP = 4
GROUP = 2
LANE = 128
VMEM_LIMIT = 56 * 1024 * 1024
SMALL_LIMIT = 24 * 1024 * 1024

TOK = 128
CHOICES = TOK * TOP
EXPERTS = 64
SLOTS = 8
OSLOTS = 2
DEVICES = 32
MAIN = EXPERTS * SLOTS
SPILL = EXPERTS * OSLOTS
ROWS = MAIN + SPILL
D = 2048
HID = 768
PIECES = 16
PIECE = 3 * LANE
HALF = PIECE // 2
KSTEP = 2
GATE = 0


def iota(shape, axis):
    return lax.broadcasted_iota(jnp.int32, shape, axis)


def ones_where(hit):
    return jnp.where(hit, 1, 0)


def spill_index(row):
    return (row >> 4) * 4 + (row & 3)


def spill_quarter(row):
    return (row >> 2) & 3


def one_hot(hit):
    return jnp.where(hit, 1.0, 0.0).astype(jnp.bfloat16)


def dot(a, b):
    return jnp.dot(a, b, preferred_element_type=jnp.float32)


def across(a, b):
    return lax.dot_general(a, b, (((1,), (1,)), ((), ())), preferred_element_type=jnp.float32)


MAIN_E = MAIN // 2
SPILL_E = SPILL // 2
ROWS_E = ROWS // 2


def dispatch_kernel(
    rows, cols, partner_r, partner_c, cap_r, cap_c, scale, tokens, out, s_hi, s_lo, p_hi, p_lo,
):
    ids_r, key_r, pick_r = rows[0:1, :], rows[1:2, :], rows[2:3, :]
    rank_r = jnp.zeros((1, CHOICES), jnp.int32)
    rank_c = []
    for b in range(TOP):
        at = slice(b * TOK, (b + 1) * TOK)
        ids_c, key_c = cols[at, 0:1], cols[at, 1:2]
        same = ids_c == ids_r
        rank_r += jnp.sum(ones_where(same & (key_c < key_r)), axis=0, keepdims=True)
        rank_c.append(jnp.sum(ones_where(same & (key_r < key_c)), axis=1, keepdims=True))
    room_r = jnp.sum(jnp.where(iota((EXPERTS, CHOICES), 0) == ids_r, cap_c[...], 0), axis=0, keepdims=True)
    mate_r = jnp.sum(
        jnp.where(iota((EXPERTS // GROUP, CHOICES), 0) == (ids_r >> 1), partner_c[...], 0), axis=0, keepdims=True
    )
    target_r = mate_r * GROUP + pick_r
    over_r = ones_where(rank_r >= room_r)
    spill_r = jnp.zeros((1, CHOICES), jnp.int32)
    main_c, lost_c = [], []
    for b in range(TOP):
        at = slice(b * TOK, (b + 1) * TOK)
        ids_c, key_c, pick_c = cols[at, 0:1], cols[at, 1:2], cols[at, 2:3]
        room_c = jnp.sum(jnp.where(iota((TOK, EXPERTS), 1) == ids_c, cap_r[...], 0), axis=1, keepdims=True)
        mate_c = jnp.sum(
            jnp.where(iota((TOK, EXPERTS // GROUP), 1) == (ids_c >> 1), partner_r[...], 0), axis=1, keepdims=True
        )
        target_c = mate_c * GROUP + pick_c
        over_c = ones_where(rank_c[b] >= room_c)
        same = target_c == target_r
        spill_r += jnp.sum(jnp.where(same & (key_c < key_r), over_c, 0), axis=0, keepdims=True)
        spill_c = jnp.sum(jnp.where(same & (key_r < key_c), over_r, 0), axis=1, keepdims=True)
        main_c.append(jnp.where(over_c == 0, ids_c * SLOTS + rank_c[b], -1))
        lost_c.append(jnp.where((over_c == 1) & (spill_c < OSLOTS), target_c * OSLOTS + spill_c, -1))
    main_r = jnp.where(over_r == 0, ids_r * SLOTS + rank_r, -1)
    lost_r = jnp.where((over_r == 1) & (spill_r < OSLOTS), target_r * OSLOTS + spill_r, -1)

    s_main = jnp.zeros((TOK, MAIN), jnp.float32)
    s_lost = jnp.zeros((TOK, MAIN), jnp.float32)
    lane = iota((TOK, MAIN), 1)
    second, own = lane >> 8, lane & (MAIN_E - 1)
    main_of = (own >> 3) * 16 + second * SLOTS + (own & 7)
    lost_of = (own >> 3) * 4 + second * OSLOTS + (own & 1)
    pick_main = jnp.zeros((MAIN, TOK), jnp.float32)
    pick_lost = jnp.zeros((MAIN, TOK), jnp.float32)
    line = iota((MAIN, TOK), 0)
    for k in range(TOP):
        at = slice(k * TOK, (k + 1) * TOK)
        weight = scale[:, k : k + 1]
        s_main += jnp.where(main_of == main_c[k], weight, 0.0)
        s_lost += jnp.where(lost_of == lost_c[k], weight, 0.0)
        pick_main += jnp.where(line == main_r[:, at], 1.0, 0.0)
        pick_lost += jnp.where(spill_index(line) == lost_r[:, at], 1.0, 0.0)
    for value, high, low in ((s_main, s_hi, s_lo), (s_lost, p_hi, p_lo)):
        top = value.astype(jnp.bfloat16)
        high[...] = top
        low[...] = (value - top.astype(jnp.float32)).astype(jnp.bfloat16)

    picks = pick_main.astype(jnp.bfloat16)
    quarter = D // 4
    packed = jnp.zeros((MAIN, quarter), jnp.float32)
    for q in range(4):
        at = slice(q * quarter, (q + 1) * quarter)
        piece = tokens[:, at]
        out[:, at] = jnp.dot(picks, piece, preferred_element_type=jnp.float32).astype(jnp.bfloat16)
        own = jnp.where(spill_quarter(line) == q, pick_lost, 0.0).astype(jnp.bfloat16)
        packed += jnp.dot(own, piece, preferred_element_type=jnp.float32)
    out[:, D:] = packed.astype(jnp.bfloat16)


def main_line(row, e):
    return (row >> 3) * 16 + e * SLOTS + (row & 7)


def packed_line(row, e, q):
    return (row >> 1) * 16 + q * 4 + e * OSLOTS + (row & 1)


def split_kernel(x, out):
    quarter = D // 4
    for e in range(2):
        shape = (MAIN_E, MAIN)
        pick = one_hot(iota(shape, 1) == main_line(iota(shape, 0), e))
        shape = (SPILL_E, MAIN)
        for q in range(4):
            at = slice(q * quarter, (q + 1) * quarter)
            out[e, :MAIN_E, at] = dot(pick, x[:, at]).astype(jnp.bfloat16)
            own = one_hot(iota(shape, 1) == packed_line(iota(shape, 0), e, q))
            out[e, MAIN_E:, at] = dot(own, x[:, D:]).astype(jnp.bfloat16)


def pack_kernel(gate, up, down, first, high, low):
    first[:LANE, :] = gate[0]
    first[LANE : 2 * LANE, :] = up[0]
    first[2 * LANE :, :] = down[0].T
    high[:LANE, :] = gate[1]
    high[LANE:, :] = up[1, : HALF - LANE]
    low[: HALF - LANE, :] = up[1, HALF - LANE :]
    low[HALF - LANE :, :] = down[1].T


WIDE = 2 * LANE
TILES = HID // WIDE


def expert(x, out, gate_w, up_w, down_w, hidden_s, copies):
    for group in copies:
        for copy in group:
            copy.start()
    for n in range(TILES):
        for copy in copies[n]:
            copy.wait()
        cut = slice(n * WIDE, (n + 1) * WIDE)
        gate = dot(x[...], gate_w[:, :, cut].reshape(D, WIDE))
        up = dot(x[...], up_w[:, :, cut].reshape(D, WIDE))
        hidden_s[:, cut] = ((gate / (1.0 + jnp.exp(-gate))) * up).astype(jnp.bfloat16)
    quarter = D // 4
    shape = (MAIN_E, SPILL_E)
    line, row = iota(shape, 0), iota(shape, 1)
    packed = jnp.zeros((MAIN_E, quarter), jnp.float32)
    for q in range(4):
        for copy in copies[TILES + q]:
            copy.wait()
        at = slice(q * quarter, (q + 1) * quarter)
        answer = across(hidden_s[...], down_w[q * 4 : (q + 1) * 4].reshape(quarter, HID)).astype(jnp.bfloat16)
        out[:, at] = answer[:MAIN_E]
        place = one_hot((((line >> 3) * 2 + (line & 1)) == row) & (((line >> 1) & 3) == q))
        packed += dot(place, answer[MAIN_E:])
    out[:, D:] = packed.astype(jnp.bfloat16)


def first_kernel(x, weights, out, gate_w, up_w, down_w, hidden_s, rows, sems, sem):
    copies = [[pltpu.make_async_copy(x.at[0], rows, sem)]] + [[] for _ in range(TILES + 3)]
    for n in range(TILES):
        cut = pl.ds(n * WIDE, WIDE)
        for i, to in enumerate((gate_w, up_w)):
            source = weights.at[:, pl.ds(i * LANE, LANE), cut]
            copies[n].append(pltpu.make_async_copy(source, to.at[:, :, cut], sems.at[i, n]))
    for q in range(4):
        own = pl.ds(q * 4, 4)
        source = weights.at[own, pl.ds(2 * LANE, LANE)]
        copies[TILES + q].append(pltpu.make_async_copy(source, down_w.at[own], sems.at[2, q]))
    expert(rows, out, gate_w, up_w, down_w, hidden_s, copies)


def second_kernel(me, x, *refs):
    highs, lows = refs[:PIECES], refs[PIECES : 2 * PIECES]
    out, gate_w, up_w, down_w, hidden_s, sems = refs[2 * PIECES :]
    copies = [[] for _ in range(TILES + 4)]
    half = HALF - LANE
    for j in range(PIECES):
        owner = lax.rem(me[0] + j, PIECES)
        moves = [
            (highs[j].at[pl.ds(0, LANE)], gate_w.at[owner]),
            (highs[j].at[pl.ds(LANE, half)], up_w.at[owner, pl.ds(0, half)]),
            (lows[j].at[pl.ds(0, half)], up_w.at[owner, pl.ds(half, half)]),
            (lows[j].at[pl.ds(half, LANE)], down_w.at[owner]),
        ]
        now = [pltpu.make_async_copy(source, to, sems.at[i, j]) for i, (source, to) in enumerate(moves)]
        copies[0] += now[:-1]
        copies[TILES] += now[-1:]
    expert(x.at[1], out, gate_w, up_w, down_w, hidden_s, copies)


def mix(e, ans, s_hi, s_lo, p_hi, p_lo):
    own = slice(e * MAIN_E, (e + 1) * MAIN_E)
    both = jnp.concatenate([s_hi[:, own], s_lo[:, own]], axis=0)
    total = dot(both, ans[:, :D])
    total = total[:TOK] + total[TOK:]
    both = jnp.concatenate([p_hi[:, own], p_lo[:, own]], axis=0)
    quarter = (iota(both.shape, 1) >> 1) & 3
    zero = jnp.zeros((), jnp.bfloat16)
    sums = []
    for q in range(4):
        lost = dot(jnp.where(quarter == q, both, zero), ans[:, D:])
        sums.append(lost[:TOK] + lost[TOK:])
    return total + jnp.concatenate(sums, axis=1)


def mix_kernel(ans, s_hi, s_lo, p_hi, p_lo, out):
    out[...] = mix(1, ans, s_hi, s_lo, p_hi, p_lo)


def final_kernel(ans, s_hi, s_lo, p_hi, p_lo, before, out):
    out[...] = (before[...] + mix(0, ans, s_hi, s_lo, p_hi, p_lo)).astype(jnp.bfloat16)


def params(size=SMALL_LIMIT):
    return pltpu.CompilerParams(vmem_limit_bytes=size)


def vmem(count):
    return [pl.BlockSpec(memory_space=pltpu.VMEM)] * count


def anywhere(count):
    return [pl.BlockSpec(memory_space=pl.ANY)] * count


SMEM = pl.BlockSpec(memory_space=pltpu.SMEM)


def cost(flops, size):
    return pl.CostEstimate(flops=flops, bytes_accessed=size, transcendentals=0)


def dispatch(expert_ids, priority, overflow_pick, partner, capacity, route_scale, tokens):
    def by_choice(block):
        return block.reshape(TOK, TOP).T.reshape(1, CHOICES)

    rows = jnp.concatenate([by_choice(expert_ids), by_choice(priority), by_choice(overflow_pick)], axis=0)
    scales = jax.ShapeDtypeStruct((TOK, MAIN), jnp.bfloat16)
    return pl.pallas_call(
        dispatch_kernel,
        out_shape=[jax.ShapeDtypeStruct((MAIN, D + D // 4), jnp.bfloat16)] + [scales] * 4,
        in_specs=vmem(8),
        out_specs=vmem(5),
        compiler_params=params(),
        cost_estimate=cost(2 * MAIN * TOK * D * 2, 4 * 1024 * 1024),
    )(
        rows, rows.T, partner[None, :], partner[:, None], capacity[None, :], capacity[:, None],
        route_scale, tokens,
    )


def pack(gate_weight, up_weight, down_weight):
    half = jax.ShapeDtypeStruct((HALF, HID), jnp.bfloat16)
    return pl.pallas_call(
        pack_kernel,
        out_shape=[jax.ShapeDtypeStruct((PIECE, HID), jnp.bfloat16), half, half],
        in_specs=vmem(3),
        out_specs=vmem(3),
        compiler_params=params(VMEM_LIMIT),
        cost_estimate=cost(0, 8 * PIECE * HID),
    )(gate_weight, up_weight, down_weight)


def split_rows(x):
    return pl.pallas_call(
        split_kernel,
        out_shape=jax.ShapeDtypeStruct((2, ROWS_E, D), jnp.bfloat16),
        in_specs=vmem(1),
        out_specs=vmem(1)[0],
        compiler_params=params(),
        cost_estimate=cost(2 * ROWS * MAIN * D, 6 * 1024 * 1024),
    )(x)


def expert_scratch():
    return [pltpu.VMEM((PIECES, LANE, HID), jnp.bfloat16)] * 3 + [pltpu.VMEM((ROWS_E, HID), jnp.bfloat16)]


EXPERT_OUT = jax.ShapeDtypeStruct((MAIN_E, D + D // 4), jnp.bfloat16)
EXPERT_COST = cost(6 * ROWS_E * D * HID, 13 * 1024 * 1024)


def first_expert(x, weights):
    return pl.pallas_call(
        first_kernel,
        out_shape=EXPERT_OUT,
        in_specs=anywhere(2),
        out_specs=vmem(1)[0],
        scratch_shapes=[
            *expert_scratch(),
            pltpu.VMEM((ROWS_E, D), jnp.bfloat16),
            pltpu.SemaphoreType.DMA((3, 4)),
            pltpu.SemaphoreType.DMA,
        ],
        compiler_params=params(VMEM_LIMIT),
        cost_estimate=EXPERT_COST,
    )(x, weights)


def second_expert(me, x, pieces):
    return pl.pallas_call(
        second_kernel,
        out_shape=EXPERT_OUT,
        in_specs=[SMEM] + vmem(1) + anywhere(len(pieces)),
        out_specs=vmem(1)[0],
        scratch_shapes=[*expert_scratch(), pltpu.SemaphoreType.DMA((4, PIECES))],
        compiler_params=params(VMEM_LIMIT),
        cost_estimate=EXPERT_COST,
    )(me, x, *pieces)


def combine(ans, scales):
    return pl.pallas_call(
        mix_kernel,
        out_shape=jax.ShapeDtypeStruct((TOK, D), jnp.float32),
        in_specs=vmem(5),
        out_specs=vmem(1)[0],
        compiler_params=params(),
        cost_estimate=cost(5 * TOK * MAIN_E * D, 3 * 1024 * 1024),
    )(ans, *scales)


def combine_last(ans, scales, before):
    return pl.pallas_call(
        final_kernel,
        out_shape=jax.ShapeDtypeStruct((TOK, D), jnp.bfloat16),
        in_specs=vmem(6),
        out_specs=vmem(1)[0],
        compiler_params=params(),
        cost_estimate=cost(5 * TOK * MAIN_E * D, 3 * 1024 * 1024),
    )(ans, *scales, before)


def exchange(block):
    rows, width = block.shape
    shaped = block.reshape(DEVICES, rows // DEVICES, width)
    return lax.all_to_all(shaped, "expert", split_axis=0, concat_axis=0, tiled=True).reshape(rows, width)


def after(value, *others):
    return lax.optimization_barrier((value, *others))[0]


def per_device(
    tokens, expert_ids, priority, overflow_pick, partner, capacity, route_scale,
    gate_weight, up_weight, down_weight,
):
    me = lax.axis_index("fsdp").astype(jnp.int32).reshape(1)
    right = [(i, (i + 1) % PIECES) for i in range(PIECES)]
    left = [(i, (i - 1) % PIECES) for i in range(PIECES)]

    own, high, low = pack(gate_weight, up_weight, down_weight)
    highs, lows = {0: high}, {0: low}
    half = PIECES // 2
    for step in range(1, half + 1):
        near_r, near_l = highs[(PIECES - step + 1) % PIECES], lows[step - 1]
        if step == GATE + 1:
            weights = lax.all_gather(after(own, near_r) if GATE else own, "fsdp")
        if step == KSTEP + 1:
            ready = after(tokens, near_r, near_l, highs[step - 1], lows[PIECES - step + 1])
            out, *scales = dispatch(expert_ids, priority, overflow_pick, partner, capacity, route_scale, ready)
            x = split_rows(exchange(out))
        highs[PIECES - step] = lax.ppermute(near_r, "fsdp", right)
        lows[step] = lax.ppermute(near_l, "fsdp", left)
        if step < half:
            highs[step] = lax.ppermute(highs[step - 1], "fsdp", left)
            lows[PIECES - step] = lax.ppermute(lows[(PIECES - step + 1) % PIECES], "fsdp", right)
    pieces = [highs[j] for j in range(PIECES)] + [lows[j] for j in range(PIECES)]

    second = second_expert(me, x, pieces)
    far = PIECES // 2 - 1
    x0 = after(x, highs[PIECES - far], lows[far])
    first = first_expert(x0, weights)
    before = combine(exchange(second), scales)
    return combine_last(exchange(first), scales, before)


def solution(mesh):
    in_specs = (
        P(("fsdp", "expert"), None),
        P(("fsdp", "expert"), None),
        P(("fsdp", "expert"), None),
        P(("fsdp", "expert"), None),
        P(),
        P(),
        P(("fsdp", "expert"), None),
        P("expert", "fsdp", None),
        P("expert", "fsdp", None),
        P("expert", None, "fsdp"),
    )
    out_specs = P(("fsdp", "expert"), None)
    return jax.shard_map(
        per_device, mesh=mesh, in_specs=in_specs, out_specs=out_specs, check_vma=False
    )
```
